512 devices in a mesh: dp: 16 (over z_lo, y), fsdp: 32 (over z_hi, x, core).
Axes of the slice: x: 4, y: 4, z: 16 (z_hi: 4, z_lo: 4; z = z_hi * 4 + z_lo), core: 2. Of those that a mesh axis runs over, the one named last changes fastest.
Arguments:
- tokens: bfloat16 [131072, 8192], P(('dp', 'fsdp')), may hold values from -6 to 6
- grad_hidden: bfloat16 [131072, 256], P(('dp', 'fsdp')), may hold values from -0.06591797 to 0.06591797
- momentum: float32 [16, 8192, 256], P('dp', 'fsdp'), may hold values from -6 to 6
- kept: int32 [16], replicated, may hold values from 0 to 63, as said below
Outputs:
- new_momentum: float32 [16, 8192, 256], P('dp', 'fsdp')
- update: float32 [8192, 256], P('fsdp')
The draws below stay inside these ranges and needn't reach their ends.
Inputs may be any that keep to these rules, and one draw needn't show every extreme that they name: `kept`: 16 different frequencies in increasing order, one fixed set used for every block; it contains 0 and 63.
All inputs are finite; a program needn't handle non-finite values.
Results may differ from the reference program's by a relative error of at most 0.019.
Values may be sent and summed in bfloat16 or wider, within the bound.
No kernel may reach another device: no remote copies, remote signals or barrier semaphores. Data moves between devices by JAX's collectives and lax.ppermute only.
A program may use at most 64 MiB of HBM per device.

```python
import math
import jax
import jax.numpy as jnp
from jax import lax

D = 8192
COLS = 256
TOK_DEV = 256
SPAN = 64
KEEP = 16
TOKENS = 131072
N_DP = 16
N_FSDP = 32


def draw_kept(key, part):
    key = jax.random.fold_in(key, 7)
    inner = jax.random.permutation(key, SPAN - 2)[:KEEP - 2].astype(jnp.int32) + 1
    inner = jnp.sort(inner)
    first = jnp.zeros((1,), jnp.int32)
    last = jnp.full((1,), SPAN - 1, jnp.int32)
    return jnp.concatenate([first, inner, last])


def levels(stream_key, extent, pieces, least, largest):
    gain = 1.0
    for dim, blocks in pieces:
        draws = jax.random.uniform(jax.random.fold_in(jax.random.fold_in(stream_key, 6), dim), (blocks,), jnp.float32, least / len(pieces), largest / len(pieces))
        gain = gain * jnp.repeat(jnp.exp(draws), extent[dim] // blocks).reshape((-1,) + (1,) * (len(extent) - 1 - dim))
    return gain


def gaussian(stream_key, shape, width, most, shards=(), dtype=jnp.bfloat16):
    values = width * jax.random.normal(stream_key, shape, jnp.float32)
    if shards:
        values = values * levels(stream_key, shape, shards, -0.22, 0.18)
    return jnp.clip(values, -most, most).astype(dtype)


def setup_inputs(seed: int = 0) -> dict:
    key_of = jax.random.split(jax.random.key(seed), 5)
    return {
        "tokens": gaussian(key_of[0], (TOKENS, D), 1.0, 6.0, ((0, 512),)),
        "grad_hidden": gaussian(key_of[1], (TOKENS, COLS), 0.011, 0.06591797, ((0, 512),)),
        "momentum": gaussian(key_of[2], (N_DP, D, COLS), 1.0, 6.0, ((0, 16), (1, 32)), jnp.float32),
        "kept": draw_kept(jax.random.fold_in(key_of[4], 71), 0),
    }


def kept_basis(kept):
    freq = kept.astype(jnp.float32)[:, None]
    place = jnp.arange(SPAN).astype(jnp.float32)[None, :]
    scale = jnp.where(kept == 0, math.sqrt(1.0 / SPAN), math.sqrt(2.0 / SPAN)).astype(jnp.float32)
    return scale[:, None] * jnp.cos(math.pi * (2.0 * place + 1.0) * freq / (2.0 * SPAN))

def reference(tokens, grad_hidden, momentum, kept):
    inputs = tokens.reshape(N_DP, N_FSDP, TOK_DEV, D)
    hiddens = grad_hidden.reshape(N_DP, N_FSDP, TOK_DEV, COLS)

    def replica(pair):

        def add_group(total, item):
            term = lax.dot_general(item[0], item[1], (((0,), (0,)), ((), ())), preferred_element_type=jnp.float32)
            rounded = lax.optimization_barrier(term.astype(jnp.bfloat16))
            return (total + rounded.astype(jnp.float32), None)
        total, _ = lax.scan(add_group, jnp.zeros((D, COLS), jnp.float32), pair)
        return total
    grads = lax.map(replica, (inputs, hiddens))
    moment = 0.9 * momentum + grads
    basis = kept_basis(kept)
    blocks = moment.reshape(N_DP, D // SPAN, SPAN, COLS // SPAN, SPAN)
    high = lax.Precision.HIGHEST
    coeffs = jnp.einsum('kn,ranbm,lm->rabkl', basis, blocks, basis, precision=high)
    back = jnp.einsum('kn,rabkl,lm->ranbm', basis, coeffs, basis, precision=high)
    new_momentum = (blocks - back).reshape(N_DP, D, COLS)
    sent = lax.optimization_barrier(coeffs.astype(jnp.bfloat16)).astype(jnp.float32)
    mean = lax.optimization_barrier(jnp.sum(sent, axis=0)) / N_DP
    update = 4.0 * jnp.einsum('kn,abkl,lm->anbm', basis, mean, basis, precision=high)
    return (new_momentum, update.reshape(D, COLS))
```

```python
import functools
import math

import jax
import jax.numpy as jnp
from jax import lax
from jax.experimental import pallas as pl
from jax.experimental.pallas import tpu as pltpu
from jax.sharding import PartitionSpec as P

SPAN = 64
KEEP = 16
UNIT = 256
RING = 4
HIGH = lax.Precision.HIGHEST
BF16 = jnp.bfloat16
F32 = jnp.float32

MASKS = ((0, 3, 1, 2), (0, 1, 3, 2))


def pairs(step):
    out = []
    for zh in range(RING):
        for x in range(RING):
            for c in range(2):
                a, b, d = step(zh, x, c)
                out.append(((zh * RING + x) * 2 + c, (a * RING + b) * 2 + d))
    return out


CORE = pairs(lambda zh, x, c: (zh, x, 1 - c))
X1 = pairs(lambda zh, x, c: (zh, x ^ MASKS[c][2], c))
X2 = pairs(lambda zh, x, c: (zh, x ^ MASKS[c][1], c))
Z1 = pairs(lambda zh, x, c: (zh ^ MASKS[c][2], x, c))
Z2 = pairs(lambda zh, x, c: (zh ^ MASKS[c][1], x, c))


def product_kernel(flip, places, me_ref, tokens_ref, hidden_ref, out_ref, held, sems):
    me = me_ref[0]
    c = me % 2
    x = (me // 2) % RING
    zh = me // (2 * RING)
    if flip:
        c = 1 - c
    copies = []
    for u, (p, q) in enumerate(places):
        mx = jnp.where(c == 0, MASKS[0][p], MASKS[1][p])
        mz = jnp.where(c == 0, MASKS[0][q], MASKS[1][q])
        block = ((zh ^ mz) * RING + (x ^ mx)) * 2 + c
        start = pl.multiple_of(block * UNIT, UNIT)
        copy = pltpu.make_async_copy(tokens_ref.at[:, pl.ds(start, UNIT)], held.at[u], sems.at[u])
        copy.start()
        copies.append(copy)
    left = hidden_ref[...].T
    for u, copy in enumerate(copies):
        copy.wait()
        out_ref[u] = jnp.dot(left, held[u], preferred_element_type=F32).astype(BF16)


def product(flip, places, me, tokens, hidden):
    n = len(places)
    toks = tokens.shape[0]
    cols = hidden.shape[1]
    return pl.pallas_call(
        functools.partial(product_kernel, flip, places),
        out_shape=jax.ShapeDtypeStruct((n, cols, UNIT), BF16),
        in_specs=[
            pl.BlockSpec(memory_space=pltpu.SMEM),
            pl.BlockSpec(memory_space=pl.ANY),
            pl.BlockSpec(memory_space=pltpu.VMEM),
        ],
        out_specs=pl.BlockSpec(memory_space=pltpu.VMEM),
        scratch_shapes=[pltpu.VMEM((n, toks, UNIT), BF16), pltpu.SemaphoreType.DMA((n,))],
        cost_estimate=pl.CostEstimate(
            flops=2 * n * toks * cols * UNIT, bytes_accessed=2 * n * UNIT * (toks + cols), transcendentals=0
        ),
    )(me, tokens, hidden)


def kept_basis(kept):
    freq = kept.astype(F32)[:, None]
    place = jnp.arange(SPAN).astype(F32)[None, :]
    scale = jnp.where(kept == 0, math.sqrt(1.0 / SPAN), math.sqrt(2.0 / SPAN)).astype(F32)
    return scale[:, None] * jnp.cos(math.pi * (2.0 * place + 1.0) * freq / (2.0 * SPAN))


def dot(a, b):
    return jnp.dot(a, b, precision=HIGH, preferred_element_type=F32)


def moment_kernel(part_ref, r1_ref, r2_ref, momentum_ref, wide_ref, tall_ref, out_ref, sent_ref):
    grad = part_ref[...].astype(F32) + r1_ref[...].astype(F32) + r2_ref[...].astype(F32)
    moment = 0.9 * momentum_ref[...] + grad.T
    wide = wide_ref[...]
    tall = tall_ref[...]
    coeffs = dot(dot(wide, moment), tall)
    half = coeffs.shape[0] // 2
    sent = jnp.concatenate([coeffs[:half], coeffs[half:]], axis=1).astype(BF16)
    for r in range(sent_ref.shape[0]):
        sent_ref[r] = sent
    out_ref[...] = moment - dot(tall, dot(coeffs, wide))


def update_kernel(every_ref, wide_ref, tall_ref, out_ref):
    total = jnp.sum(every_ref[...].astype(F32), axis=0)
    n = total.shape[1] // 2
    mean = jnp.concatenate([total[:, :n], total[:, n:]], axis=0) * (4.0 / every_ref.shape[0])
    out_ref[...] = dot(tall_ref[...], dot(mean, wide_ref[...]))


def on_device(tokens, grad_hidden, momentum, kept):
    rows = momentum.shape[1]
    cols = momentum.shape[2]
    n_dp = lax.axis_size("dp")
    me = lax.axis_index("fsdp").astype(jnp.int32).reshape(1)
    early = [(p, q) for p in range(RING) for q in (2, 3)]
    late = [(p, q) for p in range(RING) for q in (0, 1)]

    def swap(a, perm):
        return lax.ppermute(a, "fsdp", perm)

    def add(a, b):
        return (a.astype(F32) + b.astype(F32)).astype(BF16)

    other_a = product(True, early, me, tokens, grad_hidden)
    got_a = swap(other_a, CORE)
    other_b = product(True, late, me, tokens, grad_hidden)
    got_b = swap(other_b, CORE)
    own_a = product(False, early, me, tokens, grad_hidden)
    own_b = product(False, late, me, tokens, grad_hidden)

    def along_x(own, got):
        away = add(own[4:8], got[4:8])
        back = swap(away, X1)
        near = add(own[2:4].astype(F32) + got[2:4].astype(F32), back[2:4])
        last = swap(near, X2)
        return add(own[0:2].astype(F32) + got[0:2].astype(F32) + back[0:2].astype(F32), last)

    a = along_x(own_a, got_a)
    b = along_x(own_b, got_b)
    r3 = swap(a[1], Z1)
    r2 = swap(a[0], Z1)
    r1 = swap(add(b[1], r3), Z2)

    basis = kept_basis(kept)
    wide = jnp.kron(jnp.eye(cols // SPAN, dtype=F32), basis)
    tall = wide.T
    kw = wide.shape[0]
    new_momentum, sent = pl.pallas_call(
        moment_kernel,
        out_shape=(
            jax.ShapeDtypeStruct((rows, cols), F32),
            jax.ShapeDtypeStruct((n_dp, kw // 2, kw * 2), BF16),
        ),
    )(b[0], r2, r1, momentum[0], wide, tall)
    every = lax.all_to_all(sent, "dp", 0, 0, tiled=True)
    update = pl.pallas_call(update_kernel, out_shape=jax.ShapeDtypeStruct((rows, cols), F32))(every, wide, tall)
    return (new_momentum[None], update)


def solution(mesh):
    in_specs = (P(("dp", "fsdp"), None), P(("dp", "fsdp"), None), P("dp", "fsdp", None), P())
    out_specs = (P("dp", "fsdp", None), P("fsdp", None))
    return jax.shard_map(
        on_device, mesh=mesh, in_specs=in_specs, out_specs=out_specs, check_vma=False
    )
```

```python
import functools
import math

import jax
import jax.numpy as jnp
from jax import lax
from jax.experimental import pallas as pl
from jax.experimental.pallas import tpu as pltpu
from jax.sharding import PartitionSpec as P

SPAN = 64
KEEP = 16
UNIT = 256
RING = 4
VMEM_LIMIT = 8 << 20
HIGH = lax.Precision.HIGHEST
BF16 = jnp.bfloat16
F32 = jnp.float32

MASKS = ((0, 3, 1, 2), (0, 1, 3, 2))

EARLY = tuple((p, q) for p in range(RING) for q in (2, 3))
LATE = tuple((p, q) for p in range(RING) for q in (0, 1))


def pairs(step):
    out = []
    for zh in range(RING):
        for x in range(RING):
            for c in range(2):
                a, b, d = step(zh, x, c)
                out.append(((zh * RING + x) * 2 + c, (a * RING + b) * 2 + d))
    return out


CORE = pairs(lambda zh, x, c: (zh, x, 1 - c))
X1 = pairs(lambda zh, x, c: (zh, x ^ MASKS[c][2], c))
X2 = pairs(lambda zh, x, c: (zh, x ^ MASKS[c][1], c))
Z1 = pairs(lambda zh, x, c: (zh ^ MASKS[c][2], x, c))
Z2 = pairs(lambda zh, x, c: (zh ^ MASKS[c][1], x, c))

LONG = pl.CostEstimate(flops=20_000_000_000, bytes_accessed=0, transcendentals=0)
IN_VMEM = pl.BlockSpec(memory_space=pltpu.VMEM)
PARAMS = pltpu.CompilerParams(vmem_limit_bytes=VMEM_LIMIT)


def block_start(me, flip, p, q):
    c = me % 2
    x = (me // 2) % RING
    zh = me // (2 * RING)
    if flip:
        c = 1 - c
    mx = jnp.where(c == 0, MASKS[0][p], MASKS[1][p])
    mz = jnp.where(c == 0, MASKS[0][q], MASKS[1][q])
    return pl.multiple_of((((zh ^ mz) * RING + (x ^ mx)) * 2 + c) * UNIT, UNIT)


def times(left, right):
    return jnp.dot(left, right, preferred_element_type=F32).astype(BF16)


def first_kernel(places, me_ref, tokens_ref, hidden_ref, out_ref, held_ref, left_ref, hidden, sems, hidden_sem):
    of_hidden = pltpu.make_async_copy(hidden_ref, hidden, hidden_sem)
    of_hidden.start()
    copies = []
    n = sems.shape[0]
    rows = tokens_ref.shape[0] // n
    for i in range(n):
        part = pl.ds(i * rows, rows)
        copy = pltpu.make_async_copy(tokens_ref.at[part], held_ref.at[part], sems.at[i])
        copy.start()
        copies.append(copy)
    of_hidden.wait()
    left = hidden[...].T
    left_ref[...] = left
    for copy in copies:
        copy.wait()
    for u, place in enumerate(places):
        out_ref[u] = times(left, held_ref[:, pl.ds(block_start(me_ref[0], *place), UNIT)])


def first_product(places, me, tokens, grad_hidden):
    toks, cols = grad_hidden.shape
    tokens = pltpu.with_memory_space_constraint(tokens, pltpu.HBM)
    grad_hidden = pltpu.with_memory_space_constraint(grad_hidden, pltpu.HBM)
    hbm = pl.BlockSpec(memory_space=pltpu.HBM)
    return pl.pallas_call(
        functools.partial(first_kernel, places),
        out_shape=(
            pltpu.VMEM((len(places), cols, UNIT), BF16),
            pltpu.VMEM(tokens.shape, BF16),
            pltpu.VMEM((cols, toks), BF16),
        ),
        in_specs=[pl.BlockSpec(memory_space=pltpu.SMEM), hbm, hbm],
        out_specs=(IN_VMEM, IN_VMEM, IN_VMEM),
        scratch_shapes=[
            pltpu.VMEM((toks, cols), BF16),
            pltpu.SemaphoreType.DMA((4,)),
            pltpu.SemaphoreType.DMA,
        ],
        compiler_params=PARAMS,
    )(me, tokens, grad_hidden)


def product_kernel(places, me_ref, left_ref, held_ref, out_ref):
    left = left_ref[...]
    for u, place in enumerate(places):
        out_ref[u] = times(left, held_ref[:, pl.ds(block_start(me_ref[0], *place), UNIT)])


def product(places, me, left, held, cost=None):
    cols, toks = left.shape
    return pl.pallas_call(
        functools.partial(product_kernel, places),
        out_shape=pltpu.VMEM((len(places), cols, UNIT), BF16),
        in_specs=[pl.BlockSpec(memory_space=pltpu.SMEM), IN_VMEM, IN_VMEM],
        out_specs=IN_VMEM,
        compiler_params=PARAMS,
        cost_estimate=cost,
    )(me, left, held)


def add_kernel(cuts, a_ref, b_ref, *out_refs):
    at = 0
    for out_ref, n in zip(out_refs, cuts, strict=True):
        for u in range(n):
            out_ref[u] = (a_ref[at + u].astype(F32) + b_ref[at + u].astype(F32)).astype(BF16)
        at += n


def add(a, b, *cuts, cost=None):
    return pl.pallas_call(
        functools.partial(add_kernel, cuts),
        out_shape=tuple(pltpu.VMEM((n, *a.shape[1:]), BF16) for n in cuts),
        in_specs=[IN_VMEM, IN_VMEM],
        out_specs=tuple(IN_VMEM for _ in cuts),
        compiler_params=PARAMS,
        cost_estimate=cost,
    )(a, b)


def kept_basis(kept):
    freq = kept.astype(F32)[:, None]
    place = jnp.arange(SPAN).astype(F32)[None, :]
    scale = jnp.where(kept == 0, math.sqrt(1.0 / SPAN), math.sqrt(2.0 / SPAN)).astype(F32)
    return scale[:, None] * jnp.cos(math.pi * (2.0 * place + 1.0) * freq / (2.0 * SPAN))


def dot(a, b):
    return jnp.dot(a, b, precision=HIGH, preferred_element_type=F32)


def block_basis(basis, blocks):
    k, n = basis.shape
    wide = jnp.concatenate([jnp.concatenate([basis] * blocks, axis=1)] * blocks, axis=0)
    row = lax.broadcasted_iota(jnp.int32, wide.shape, 0) // k
    col = lax.broadcasted_iota(jnp.int32, wide.shape, 1) // n
    return jnp.where(row == col, wide, 0.0)


def moment_kernel(part_ref, r1_ref, r2_ref, momentum_ref, basis_ref, moment_ref, coeffs_ref, sent_ref):
    grad = part_ref[0].astype(F32) + r1_ref[0].astype(F32) + r2_ref[0].astype(F32)
    moment = 0.9 * momentum_ref[0] + grad.T
    wide = block_basis(basis_ref[...], moment.shape[0] // SPAN)
    coeffs = dot(dot(wide, moment), wide.T)
    half = coeffs.shape[0] // 2
    sent = jnp.concatenate([coeffs[:half], coeffs[half:]], axis=1).astype(BF16)
    for r in range(sent_ref.shape[0]):
        sent_ref[r] = sent
    moment_ref[...] = moment
    coeffs_ref[...] = coeffs


def update_kernel(every_ref, moment_ref, coeffs_ref, basis_ref, out_ref, update_ref):
    total = jnp.sum(every_ref[...].astype(F32), axis=0)
    n = total.shape[1] // 2
    mean = jnp.concatenate([total[:, :n], total[:, n:]], axis=0) * (4.0 / every_ref.shape[0])
    wide = block_basis(basis_ref[...], out_ref.shape[1] // SPAN)
    tall = wide.T
    update_ref[...] = dot(tall, dot(mean, wide))
    out_ref[0] = moment_ref[...] - dot(tall, dot(coeffs_ref[...], wide))


def after(a, *others):
    return lax.optimization_barrier((a, *others))[0]


def on_device(tokens, grad_hidden, momentum, kept):
    rows = momentum.shape[1]
    cols = momentum.shape[2]
    n_dp = lax.axis_size("dp")
    me = lax.axis_index("fsdp").astype(jnp.int32).reshape(1)

    def swap(a, perm):
        return lax.ppermute(a, "fsdp", perm)

    def places(flip, group):
        return tuple((flip, p, q) for p, q in group)

    other_a, held, left = first_product(places(True, EARLY), me, tokens, grad_hidden)
    got_a = swap(other_a, CORE)
    own_a = product(places(False, EARLY), me, left, held)
    near, away = add(own_a, got_a, 4, 4)
    back = swap(away, X1)
    left_b = after(left, away)
    got_b = swap(product(places(True, LATE), me, left_b, held, LONG), CORE)
    own_b = product(places(False, LATE), me, left_b, held, LONG)
    near, away = add(near, back, 2, 2)
    first_away = away
    a2, a3 = add(near, swap(away, X2), 1, 1, cost=LONG)
    near, away = add(own_b, after(got_b, first_away), 4, 4)
    near, away = add(near, swap(away, X1), 2, 2)
    r3 = swap(a3, Z1)
    r2 = swap(after(a2, away), Z1)
    b0, b1 = add(near, swap(away, X2), 1, 1)
    (b1,) = add(b1, r3, 1)
    r1 = swap(b1, Z2)

    basis = kept_basis(kept)
    kw = cols // SPAN * KEEP
    moment, coeffs, sent = pl.pallas_call(
        moment_kernel,
        out_shape=(
            pltpu.VMEM((rows, cols), F32),
            pltpu.VMEM((kw, kw), F32),
            pltpu.VMEM((n_dp, kw // 2, kw * 2), BF16),
        ),
        in_specs=[IN_VMEM] * 5,
        out_specs=(IN_VMEM,) * 3,
        compiler_params=PARAMS,
    )(b0, r2, r1, momentum, basis)
    every = lax.all_to_all(sent, "dp", 0, 0, tiled=True)
    return pl.pallas_call(
        update_kernel,
        out_shape=(jax.ShapeDtypeStruct((1, rows, cols), F32), jax.ShapeDtypeStruct((rows, cols), F32)),
        in_specs=[IN_VMEM] * 4,
        out_specs=(IN_VMEM,) * 2,
        compiler_params=PARAMS,
    )(every, moment, coeffs, basis)


def solution(mesh):
    in_specs = (P(("dp", "fsdp"), None), P(("dp", "fsdp"), None), P("dp", "fsdp", None), P())
    out_specs = (P("dp", "fsdp", None), P("fsdp", None))
    return jax.shard_map(
        on_device, mesh=mesh, in_specs=in_specs, out_specs=out_specs, check_vma=False
    )
```

```python
import functools
import math

import jax
import jax.numpy as jnp
from jax import lax
from jax.experimental import pallas as pl
from jax.experimental.pallas import tpu as pltpu
from jax.sharding import PartitionSpec as P

SPAN = 64
KEEP = 16
UNIT = 256
RING = 4
VMEM_LIMIT = 8 << 20
HIGH = lax.Precision.HIGHEST
BF16 = jnp.bfloat16
F32 = jnp.float32

MASKS = ((0, 3, 1, 2), (0, 1, 3, 2))

FIRST = tuple((p, q) for p in (2, 3) for q in (2, 3))
REST = tuple((p, q) for p in (0, 1) for q in (2, 3)) + tuple((p, q) for p in range(RING) for q in (0, 1))


def pairs(step):
    out = []
    for zh in range(RING):
        for x in range(RING):
            for c in range(2):
                a, b, d = step(zh, x, c)
                out.append(((zh * RING + x) * 2 + c, (a * RING + b) * 2 + d))
    return out


CORE = pairs(lambda zh, x, c: (zh, x, 1 - c))
X1 = pairs(lambda zh, x, c: (zh, x ^ MASKS[c][2], c))
X2 = pairs(lambda zh, x, c: (zh, x ^ MASKS[c][1], c))
Z1 = pairs(lambda zh, x, c: (zh ^ MASKS[c][2], x, c))
Z2 = pairs(lambda zh, x, c: (zh ^ MASKS[c][1], x, c))

LONG = pl.CostEstimate(flops=20_000_000_000, bytes_accessed=0, transcendentals=0)
IN_VMEM = pl.BlockSpec(memory_space=pltpu.VMEM)
PARAMS = pltpu.CompilerParams(vmem_limit_bytes=VMEM_LIMIT)


def block_start(me, flip, p, q):
    c = me % 2
    x = (me // 2) % RING
    zh = me // (2 * RING)
    if flip:
        c = 1 - c
    mx = jnp.where(c == 0, MASKS[0][p], MASKS[1][p])
    mz = jnp.where(c == 0, MASKS[0][q], MASKS[1][q])
    return pl.multiple_of((((zh ^ mz) * RING + (x ^ mx)) * 2 + c) * UNIT, UNIT)


def times(left, right):
    return jnp.dot(left, right, preferred_element_type=F32).astype(BF16)


def first_kernel(places, me_ref, tokens_ref, hidden_ref, out_ref, held_ref, left_ref, hidden, sems, hidden_sem):
    of_hidden = pltpu.make_async_copy(hidden_ref, hidden, hidden_sem)
    of_hidden.start()
    copies = []
    n = sems.shape[0]
    rows = tokens_ref.shape[0] // n
    for i in range(n):
        part = pl.ds(i * rows, rows)
        copy = pltpu.make_async_copy(tokens_ref.at[part], held_ref.at[part], sems.at[i])
        copy.start()
        copies.append(copy)
    of_hidden.wait()
    left = hidden[...].T
    left_ref[...] = left
    for copy in copies:
        copy.wait()
    for u, place in enumerate(places):
        out_ref[u] = times(left, held_ref[:, pl.ds(block_start(me_ref[0], *place), UNIT)])


def first_product(places, me, tokens, grad_hidden):
    toks, cols = grad_hidden.shape
    tokens = pltpu.with_memory_space_constraint(tokens, pltpu.HBM)
    grad_hidden = pltpu.with_memory_space_constraint(grad_hidden, pltpu.HBM)
    hbm = pl.BlockSpec(memory_space=pltpu.HBM)
    return pl.pallas_call(
        functools.partial(first_kernel, places),
        out_shape=(
            pltpu.VMEM((len(places), cols, UNIT), BF16),
            pltpu.VMEM(tokens.shape, BF16),
            pltpu.VMEM((cols, toks), BF16),
        ),
        in_specs=[pl.BlockSpec(memory_space=pltpu.SMEM), hbm, hbm],
        out_specs=(IN_VMEM, IN_VMEM, IN_VMEM),
        scratch_shapes=[
            pltpu.VMEM((toks, cols), BF16),
            pltpu.SemaphoreType.DMA((4,)),
            pltpu.SemaphoreType.DMA,
        ],
        compiler_params=PARAMS,
    )(me, tokens, grad_hidden)


def product_kernel(places, me_ref, left_ref, held_ref, out_ref):
    left = left_ref[...]
    for u, place in enumerate(places):
        out_ref[u] = times(left, held_ref[:, pl.ds(block_start(me_ref[0], *place), UNIT)])


def product(places, me, left, held, cost=None):
    cols, toks = left.shape
    return pl.pallas_call(
        functools.partial(product_kernel, places),
        out_shape=pltpu.VMEM((len(places), cols, UNIT), BF16),
        in_specs=[pl.BlockSpec(memory_space=pltpu.SMEM), IN_VMEM, IN_VMEM],
        out_specs=IN_VMEM,
        compiler_params=PARAMS,
        cost_estimate=cost,
    )(me, left, held)


def add_kernel(offsets, cuts, *refs):
    in_refs, out_refs = refs[: len(offsets)], refs[len(offsets) :]
    at = 0
    for out_ref, n in zip(out_refs, cuts, strict=True):
        for u in range(n):
            total = in_refs[0][offsets[0] + at + u].astype(F32)
            for in_ref, offset in zip(in_refs[1:], offsets[1:], strict=True):
                total += in_ref[offset + at + u].astype(F32)
            out_ref[u] = total.astype(BF16)
        at += n


def add(terms, cuts, cost=None):
    arrays, offsets = zip(*terms, strict=True)
    return pl.pallas_call(
        functools.partial(add_kernel, offsets, cuts),
        out_shape=tuple(pltpu.VMEM((n, *arrays[0].shape[1:]), BF16) for n in cuts),
        in_specs=[IN_VMEM] * len(arrays),
        out_specs=tuple(IN_VMEM for _ in cuts),
        compiler_params=PARAMS,
        cost_estimate=cost,
    )(*arrays)


def kept_basis(kept):
    freq = kept.astype(F32)[:, None]
    place = jnp.arange(SPAN).astype(F32)[None, :]
    scale = jnp.where(kept == 0, math.sqrt(1.0 / SPAN), math.sqrt(2.0 / SPAN)).astype(F32)
    return scale[:, None] * jnp.cos(math.pi * (2.0 * place + 1.0) * freq / (2.0 * SPAN))


def dot(a, b):
    return jnp.dot(a, b, precision=HIGH, preferred_element_type=F32)


def block_basis(basis, blocks):
    k, n = basis.shape
    wide = jnp.concatenate([jnp.concatenate([basis] * blocks, axis=1)] * blocks, axis=0)
    row = lax.broadcasted_iota(jnp.int32, wide.shape, 0) // k
    col = lax.broadcasted_iota(jnp.int32, wide.shape, 1) // n
    return jnp.where(row == col, wide, 0.0)


def coeffs_of(basis, moment):
    wide = block_basis(basis, moment.shape[0] // SPAN)
    coeffs = dot(dot(wide, moment), wide.T)
    half = coeffs.shape[0] // 2
    return coeffs, jnp.concatenate([coeffs[:half], coeffs[half:]], axis=1)


def late_kernel(near_ref, away_ref, back_ref, basis_ref, near_out_ref, coeffs_ref):
    near_out_ref[0] = (near_ref[0].astype(F32) + back_ref[0].astype(F32)).astype(BF16)
    away = (away_ref[0].astype(F32) + back_ref[1].astype(F32)).astype(BF16)
    coeffs_ref[...] = coeffs_of(basis_ref[...], away.astype(F32).T)[1]


def near_kernel(near_ref, back_ref, momentum_ref, basis_ref, moment_ref, coeffs_ref):
    moment = 0.9 * momentum_ref[0] + (near_ref[0].astype(F32) + back_ref[0].astype(F32)).T
    moment_ref[...] = moment
    coeffs_ref[...] = coeffs_of(basis_ref[...], moment)[1]


def sent_kernel(a_ref, b_ref, sent_ref):
    sent = (a_ref[...] + b_ref[...]).astype(BF16)
    for r in range(sent_ref.shape[0]):
        sent_ref[r] = sent


def new_kernel(moment_ref, back_ref, basis_ref, out_ref):
    moment = moment_ref[...] + back_ref[0].astype(F32).T
    basis = basis_ref[...]
    wide = block_basis(basis, moment.shape[1] // SPAN)
    out_ref[0] = moment - dot(wide.T, dot(coeffs_of(basis, moment)[0], wide))


def update_kernel(every_ref, basis_ref, update_ref):
    total = jnp.sum(every_ref[...].astype(F32), axis=0)
    n = total.shape[1] // 2
    mean = jnp.concatenate([total[:, :n], total[:, n:]], axis=0) * (4.0 / every_ref.shape[0])
    wide = block_basis(basis_ref[...], update_ref.shape[1] // SPAN)
    update_ref[...] = dot(wide.T, dot(mean, wide))


def on_vmem(kernel, out_shape, *args, cost=None):
    return pl.pallas_call(
        kernel,
        out_shape=out_shape,
        in_specs=[IN_VMEM] * len(args),
        out_specs=jax.tree.map(lambda _: IN_VMEM, out_shape),
        compiler_params=PARAMS,
        cost_estimate=cost,
    )(*args)


def after(a, *others):
    return lax.optimization_barrier((a, *others))[0]


def on_device(tokens, grad_hidden, momentum, kept):
    rows = momentum.shape[1]
    cols = momentum.shape[2]
    n_dp = lax.axis_size("dp")
    me = lax.axis_index("fsdp").astype(jnp.int32).reshape(1)

    def swap(a, perm):
        return lax.ppermute(a, "fsdp", perm)

    def places(flip, group):
        return tuple((flip, p, q) for p, q in group)

    got, held, left = first_product(places(True, FIRST), me, tokens, grad_hidden)
    got = swap(got, CORE)
    own = product(places(False, FIRST), me, left, held)
    (away,) = add([(own, 0), (got, 0)], (4,))
    back = swap(away, X1)
    left = after(left, away)
    got = swap(product(places(True, REST), me, left, held, LONG), CORE)
    own = product(places(False, REST), me, left, held, LONG)
    near, away = add([(own, 0), (got, 0), (back, 0)], (2, 2))
    back = swap(away, X2)
    (late_away,) = add([(own, 8), (after(got, away), 8)], (4,), LONG)
    late_back = swap(late_away, X1)
    a2, a3 = add([(near, 0), (back, 0)], (1, 1), LONG)
    r3 = swap(a3, Z1)
    near, away = add([(own, 4), (got, 4), (after(late_back, a3), 0)], (2, 2))
    late_back = swap(away, X2)
    r2 = swap(after(a2, away), Z1)
    (away,) = add([(near, 1), (r3, 0)], (1,), LONG)

    basis = kept_basis(kept)
    kw = cols // SPAN * KEEP
    packed = pltpu.VMEM((kw // 2, kw * 2), F32)
    unit = pltpu.VMEM(away.shape, BF16)
    b0, coeffs1 = on_vmem(late_kernel, (unit, packed), near, away, late_back, basis)
    (away,) = add([(away, 0), (after(late_back, coeffs1), 1)], (1,), LONG)
    coeffs1 = swap(coeffs1, Z2)
    moment, coeffs0 = on_vmem(near_kernel, (pltpu.VMEM((rows, cols), F32), packed), b0, r2, momentum, basis)
    r1 = swap(away, Z2)
    sent = on_vmem(sent_kernel, pltpu.VMEM((n_dp, kw // 2, kw * 2), BF16), coeffs0, coeffs1, cost=LONG)
    every = lax.all_to_all(sent, "dp", 0, 0, tiled=True)
    new_momentum = on_vmem(new_kernel, jax.ShapeDtypeStruct((1, rows, cols), F32), moment, r1, basis, cost=LONG)
    update = on_vmem(update_kernel, jax.ShapeDtypeStruct((rows, cols), F32), every, basis)
    return new_momentum, update


def solution(mesh):
    in_specs = (P(("dp", "fsdp"), None), P(("dp", "fsdp"), None), P("dp", "fsdp", None), P())
    out_specs = (P("dp", "fsdp", None), P("fsdp", None))
    return jax.shard_map(
        on_device, mesh=mesh, in_specs=in_specs, out_specs=out_specs, check_vma=False
    )
```

```python
import functools
import math

import jax
import jax.numpy as jnp
from jax import lax
from jax.experimental import pallas as pl
from jax.experimental.pallas import tpu as pltpu
from jax.sharding import PartitionSpec as P

SPAN = 64
KEEP = 16
UNIT = 256
RING = 4
VMEM_LIMIT = 8 << 20
HIGH = lax.Precision.HIGHEST
BF16 = jnp.bfloat16
F32 = jnp.float32

MASKS = ((0, 3, 1, 2), (0, 1, 3, 2))

EARLY = tuple((p, q) for p in (2, 3) for q in (3, 2))
LATE = tuple((p, q) for p in (2, 3) for q in (0, 1))
REST = tuple((p, q) for p in (0, 1) for q in (3, 2)) + tuple((p, q) for p in (0, 1) for q in (0, 1))


def pairs(step):
    out = []
    for zh in range(RING):
        for x in range(RING):
            for c in range(2):
                a, b, d = step(zh, x, c)
                out.append(((zh * RING + x) * 2 + c, (a * RING + b) * 2 + d))
    return out


CORE = pairs(lambda zh, x, c: (zh, x, 1 - c))
X1 = pairs(lambda zh, x, c: (zh, x ^ MASKS[c][2], c))
X2 = pairs(lambda zh, x, c: (zh, x ^ MASKS[c][1], c))
Z1 = pairs(lambda zh, x, c: (zh ^ MASKS[c][2], x, c))
Z2 = pairs(lambda zh, x, c: (zh ^ MASKS[c][1], x, c))

LONG = pl.CostEstimate(flops=20_000_000_000, bytes_accessed=0, transcendentals=0)
IN_VMEM = pl.BlockSpec(memory_space=pltpu.VMEM)
PARAMS = pltpu.CompilerParams(vmem_limit_bytes=VMEM_LIMIT)


def block_start(me, flip, p, q):
    c = me % 2
    x = (me // 2) % RING
    zh = me // (2 * RING)
    if flip:
        c = 1 - c
    mx = jnp.where(c == 0, MASKS[0][p], MASKS[1][p])
    mz = jnp.where(c == 0, MASKS[0][q], MASKS[1][q])
    return pl.multiple_of((((zh ^ mz) * RING + (x ^ mx)) * 2 + c) * UNIT, UNIT)


def times(left, right):
    return jnp.dot(left, right, preferred_element_type=F32).astype(BF16)


def first_kernel(places, me_ref, tokens_ref, hidden_ref, out_ref, held_ref, left_ref, hidden, sems, hidden_sem):
    of_hidden = pltpu.make_async_copy(hidden_ref, hidden, hidden_sem)
    of_hidden.start()
    copies = []
    n = sems.shape[0]
    rows = tokens_ref.shape[0] // n
    for i in range(n):
        part = pl.ds(i * rows, rows)
        copy = pltpu.make_async_copy(tokens_ref.at[part], held_ref.at[part], sems.at[i])
        copy.start()
        copies.append(copy)
    of_hidden.wait()
    left = hidden[...].T
    left_ref[...] = left
    for copy in copies:
        copy.wait()
    for u, place in enumerate(places):
        out_ref[u] = times(left, held_ref[:, pl.ds(block_start(me_ref[0], *place), UNIT)])


def first_product(places, me, tokens, grad_hidden):
    toks, cols = grad_hidden.shape
    tokens = pltpu.with_memory_space_constraint(tokens, pltpu.HBM)
    grad_hidden = pltpu.with_memory_space_constraint(grad_hidden, pltpu.HBM)
    hbm = pl.BlockSpec(memory_space=pltpu.HBM)
    return pl.pallas_call(
        functools.partial(first_kernel, places),
        out_shape=(
            pltpu.VMEM((len(places), cols, UNIT), BF16),
            pltpu.VMEM(tokens.shape, BF16),
            pltpu.VMEM((cols, toks), BF16),
        ),
        in_specs=[pl.BlockSpec(memory_space=pltpu.SMEM), hbm, hbm],
        out_specs=(IN_VMEM, IN_VMEM, IN_VMEM),
        scratch_shapes=[
            pltpu.VMEM((toks, cols), BF16),
            pltpu.SemaphoreType.DMA((4,)),
            pltpu.SemaphoreType.DMA,
        ],
        compiler_params=PARAMS,
    )(me, tokens, grad_hidden)


def product_kernel(places, me_ref, left_ref, held_ref, out_ref):
    left = left_ref[...]
    for u, place in enumerate(places):
        out_ref[u] = times(left, held_ref[:, pl.ds(block_start(me_ref[0], *place), UNIT)])


def product(places, me, left, held, cost=None):
    cols, toks = left.shape
    return pl.pallas_call(
        functools.partial(product_kernel, places),
        out_shape=pltpu.VMEM((len(places), cols, UNIT), BF16),
        in_specs=[pl.BlockSpec(memory_space=pltpu.SMEM), IN_VMEM, IN_VMEM],
        out_specs=IN_VMEM,
        compiler_params=PARAMS,
        cost_estimate=cost,
    )(me, left, held)


def add_kernel(offsets, cuts, *refs):
    in_refs, out_refs = refs[: len(offsets)], refs[len(offsets) :]
    at = 0
    for out_ref, n in zip(out_refs, cuts, strict=True):
        for u in range(n):
            total = in_refs[0][offsets[0] + at + u].astype(F32)
            for in_ref, offset in zip(in_refs[1:], offsets[1:], strict=True):
                total += in_ref[offset + at + u].astype(F32)
            out_ref[u] = total.astype(BF16)
        at += n


def add(terms, cuts, cost=None):
    arrays, offsets = zip(*terms, strict=True)
    return pl.pallas_call(
        functools.partial(add_kernel, offsets, cuts),
        out_shape=tuple(pltpu.VMEM((n, *arrays[0].shape[1:]), BF16) for n in cuts),
        in_specs=[IN_VMEM] * len(arrays),
        out_specs=tuple(IN_VMEM for _ in cuts),
        compiler_params=PARAMS,
        cost_estimate=cost,
    )(*arrays)


def kept_basis(kept):
    freq = kept.astype(F32)[:, None]
    place = jnp.arange(SPAN).astype(F32)[None, :]
    scale = jnp.where(kept == 0, math.sqrt(1.0 / SPAN), math.sqrt(2.0 / SPAN)).astype(F32)
    return scale[:, None] * jnp.cos(math.pi * (2.0 * place + 1.0) * freq / (2.0 * SPAN))


def dot(a, b):
    return jnp.dot(a, b, precision=HIGH, preferred_element_type=F32)


def block_basis(basis, blocks):
    k, n = basis.shape
    wide = jnp.concatenate([jnp.concatenate([basis] * blocks, axis=1)] * blocks, axis=0)
    row = lax.broadcasted_iota(jnp.int32, wide.shape, 0) // k
    col = lax.broadcasted_iota(jnp.int32, wide.shape, 1) // n
    return jnp.where(row == col, wide, 0.0)


def coeffs_of(basis, moment):
    wide = block_basis(basis, moment.shape[0] // SPAN)
    coeffs = dot(dot(wide, moment), wide.T)
    half = coeffs.shape[0] // 2
    return coeffs, jnp.concatenate([coeffs[:half], coeffs[half:]], axis=1)


def late_kernel(near_ref, away_ref, back_ref, basis_ref, near_out_ref, coeffs_ref):
    near_out_ref[0] = (near_ref[0].astype(F32) + back_ref[0].astype(F32)).astype(BF16)
    away = (away_ref[0].astype(F32) + back_ref[1].astype(F32)).astype(BF16)
    coeffs_ref[...] = coeffs_of(basis_ref[...], away.astype(F32).T)[1]


def near_kernel(near_ref, back_ref, momentum_ref, basis_ref, moment_ref, coeffs_ref):
    moment = 0.9 * momentum_ref[0] + (near_ref[0].astype(F32) + back_ref[0].astype(F32)).T
    moment_ref[...] = moment
    coeffs_ref[...] = coeffs_of(basis_ref[...], moment)[1]


def sent_kernel(a_ref, b_ref, sent_ref):
    sent = (a_ref[...] + b_ref[...]).astype(BF16)
    for r in range(sent_ref.shape[0]):
        sent_ref[r] = sent


def new_kernel(moment_ref, back_ref, basis_ref, out_ref):
    moment = moment_ref[...] + back_ref[0].astype(F32).T
    basis = basis_ref[...]
    wide = block_basis(basis, moment.shape[1] // SPAN)
    out_ref[0] = moment - dot(wide.T, dot(coeffs_of(basis, moment)[0], wide))


def update_kernel(every_ref, basis_ref, update_ref):
    total = jnp.sum(every_ref[...].astype(F32), axis=0)
    n = total.shape[1] // 2
    mean = jnp.concatenate([total[:, :n], total[:, n:]], axis=0) * (4.0 / every_ref.shape[0])
    wide = block_basis(basis_ref[...], update_ref.shape[1] // SPAN)
    update_ref[...] = dot(wide.T, dot(mean, wide))


def on_vmem(kernel, out_shape, *args, cost=None):
    return pl.pallas_call(
        kernel,
        out_shape=out_shape,
        in_specs=[IN_VMEM] * len(args),
        out_specs=jax.tree.map(lambda _: IN_VMEM, out_shape),
        compiler_params=PARAMS,
        cost_estimate=cost,
    )(*args)


def after(a, *others):
    return lax.optimization_barrier((a, *others))[0]


def on_device(tokens, grad_hidden, momentum, kept):
    rows = momentum.shape[1]
    cols = momentum.shape[2]
    n_dp = lax.axis_size("dp")
    me = lax.axis_index("fsdp").astype(jnp.int32).reshape(1)

    def swap(a, perm):
        return lax.ppermute(a, "fsdp", perm)

    def places(flip, group):
        return tuple((flip, p, q) for p, q in group)

    got, held, left = first_product(places(True, EARLY + LATE), me, tokens, grad_hidden)
    got = swap(got, CORE)
    own = product(places(False, EARLY + LATE), me, left, held)
    (early_away,) = add([(own, 0), (got, 0)], (4,))
    early_back = swap(early_away, X1)
    left = after(left, early_away)
    other = product(places(True, REST), me, left, held, LONG)
    got_rest = swap(other, CORE)
    (late_away,) = add([(own, 4), (after(got, other), 4)], (4,))
    late_back = swap(late_away, X1)
    own = product(places(False, REST), me, after(left, late_away), held, LONG)
    near3, near2, away3, away2 = add([(own, 0), (got_rest, 0), (early_back, 0)], (1, 1, 1, 1))
    back3 = swap(away3, X2)
    back2 = swap(away2, X2)
    (a3,) = add([(near3, 0), (back3, 0)], (1,))
    r3 = swap(a3, Z1)
    near, away = add([(own, 4), (got_rest, 4), (after(late_back, a3), 0)], (2, 2))
    late_back = swap(away, X2)
    (a2,) = add([(near2, 0), (after(back2, away), 0)], (1,))
    r2 = swap(a2, Z1)
    (away,) = add([(near, 1), (r3, 0)], (1,), LONG)

    basis = kept_basis(kept)
    kw = cols // SPAN * KEEP
    packed = pltpu.VMEM((kw // 2, kw * 2), F32)
    unit = pltpu.VMEM(away.shape, BF16)
    b0, coeffs1 = on_vmem(late_kernel, (unit, packed), near, away, late_back, basis)
    (away,) = add([(away, 0), (after(late_back, coeffs1), 1)], (1,), LONG)
    coeffs1 = swap(coeffs1, Z2)
    moment, coeffs0 = on_vmem(near_kernel, (pltpu.VMEM((rows, cols), F32), packed), b0, r2, momentum, basis)
    r1 = swap(away, Z2)
    sent = on_vmem(sent_kernel, pltpu.VMEM((n_dp, kw // 2, kw * 2), BF16), coeffs0, coeffs1, cost=LONG)
    every = lax.all_to_all(sent, "dp", 0, 0, tiled=True)
    new_momentum = on_vmem(new_kernel, jax.ShapeDtypeStruct((1, rows, cols), F32), moment, r1, basis, cost=LONG)
    update = on_vmem(update_kernel, jax.ShapeDtypeStruct((rows, cols), F32), every, basis)
    return new_momentum, update


def solution(mesh):
    in_specs = (P(("dp", "fsdp"), None), P(("dp", "fsdp"), None), P("dp", "fsdp", None), P())
    out_specs = (P("dp", "fsdp", None), P("fsdp", None))
    return jax.shard_map(
        on_device, mesh=mesh, in_specs=in_specs, out_specs=out_specs, check_vma=False
    )
```

```python
import functools
import math

import jax
import jax.numpy as jnp
from jax import lax
from jax.experimental import pallas as pl
from jax.experimental.pallas import tpu as pltpu
from jax.sharding import PartitionSpec as P

SPAN = 64
KEEP = 16
UNIT = 256
RING = 4
VMEM_LIMIT = 8 << 20
HIGH = lax.Precision.HIGHEST
BF16 = jnp.bfloat16
F32 = jnp.float32

MASKS = ((0, 3, 1, 2), (0, 1, 3, 2))

EARLY = tuple((p, q) for p in (2, 3) for q in (3, 2))
LATE = tuple((p, q) for p in (2, 3) for q in (0, 1))
REST = tuple((p, q) for p in (0, 1) for q in (3, 2)) + tuple((p, q) for p in (0, 1) for q in (0, 1))


def pairs(step):
    out = []
    for zh in range(RING):
        for x in range(RING):
            for c in range(2):
                a, b, d = step(zh, x, c)
                out.append(((zh * RING + x) * 2 + c, (a * RING + b) * 2 + d))
    return out


CORE = pairs(lambda zh, x, c: (zh, x, 1 - c))
X1 = pairs(lambda zh, x, c: (zh, x ^ MASKS[1 - c][2], c))
X2 = pairs(lambda zh, x, c: (zh, x ^ MASKS[1 - c][1], c))
Z1 = pairs(lambda zh, x, c: (zh ^ MASKS[c][2], x, c))
Z2 = pairs(lambda zh, x, c: (zh ^ MASKS[c][1], x, c))

LONG = pl.CostEstimate(flops=20_000_000_000, bytes_accessed=0, transcendentals=0)
IN_VMEM = pl.BlockSpec(memory_space=pltpu.VMEM)
PARAMS = pltpu.CompilerParams(vmem_limit_bytes=VMEM_LIMIT)


def block_start(me, flip, p, q):
    c = me % 2
    x = (me // 2) % RING
    zh = me // (2 * RING)
    if flip:
        c = 1 - c
    mx = jnp.where(c == 0, MASKS[1][p], MASKS[0][p])
    mz = jnp.where(c == 0, MASKS[0][q], MASKS[1][q])
    return pl.multiple_of((((zh ^ mz) * RING + (x ^ mx)) * 2 + c) * UNIT, UNIT)


def times(left, right):
    return jnp.dot(left, right, preferred_element_type=F32).astype(BF16)


def first_kernel(places, me_ref, tokens_ref, hidden_ref, out_ref, held_ref, left_ref, hidden, sems, hidden_sem):
    of_hidden = pltpu.make_async_copy(hidden_ref, hidden, hidden_sem)
    of_hidden.start()
    copies = []
    n = sems.shape[0]
    rows = tokens_ref.shape[0] // n
    for i in range(n):
        part = pl.ds(i * rows, rows)
        copy = pltpu.make_async_copy(tokens_ref.at[part], held_ref.at[part], sems.at[i])
        copy.start()
        copies.append(copy)
    of_hidden.wait()
    left = hidden[...].T
    left_ref[...] = left
    for copy in copies:
        copy.wait()
    for u, place in enumerate(places):
        out_ref[u] = times(left, held_ref[:, pl.ds(block_start(me_ref[0], *place), UNIT)])


def first_product(places, me, tokens, grad_hidden):
    toks, cols = grad_hidden.shape
    tokens = pltpu.with_memory_space_constraint(tokens, pltpu.HBM)
    grad_hidden = pltpu.with_memory_space_constraint(grad_hidden, pltpu.HBM)
    hbm = pl.BlockSpec(memory_space=pltpu.HBM)
    return pl.pallas_call(
        functools.partial(first_kernel, places),
        out_shape=(
            pltpu.VMEM((len(places), cols, UNIT), BF16),
            pltpu.VMEM(tokens.shape, BF16),
            pltpu.VMEM((cols, toks), BF16),
        ),
        in_specs=[pl.BlockSpec(memory_space=pltpu.SMEM), hbm, hbm],
        out_specs=(IN_VMEM, IN_VMEM, IN_VMEM),
        scratch_shapes=[
            pltpu.VMEM((toks, cols), BF16),
            pltpu.SemaphoreType.DMA((4,)),
            pltpu.SemaphoreType.DMA,
        ],
        compiler_params=PARAMS,
    )(me, tokens, grad_hidden)


def product_kernel(places, me_ref, left_ref, held_ref, out_ref):
    left = left_ref[...]
    for u, place in enumerate(places):
        out_ref[u] = times(left, held_ref[:, pl.ds(block_start(me_ref[0], *place), UNIT)])


def product(places, me, left, held, cost=None):
    cols, toks = left.shape
    return pl.pallas_call(
        functools.partial(product_kernel, places),
        out_shape=pltpu.VMEM((len(places), cols, UNIT), BF16),
        in_specs=[pl.BlockSpec(memory_space=pltpu.SMEM), IN_VMEM, IN_VMEM],
        out_specs=IN_VMEM,
        compiler_params=PARAMS,
        cost_estimate=cost,
    )(me, left, held)


def add_kernel(offsets, cuts, *refs):
    in_refs, out_refs = refs[: len(offsets)], refs[len(offsets) :]
    at = 0
    for out_ref, n in zip(out_refs, cuts, strict=True):
        for u in range(n):
            total = in_refs[0][offsets[0] + at + u].astype(F32)
            for in_ref, offset in zip(in_refs[1:], offsets[1:], strict=True):
                total += in_ref[offset + at + u].astype(F32)
            out_ref[u] = total.astype(BF16)
        at += n


def add(terms, cuts, cost=None):
    arrays, offsets = zip(*terms, strict=True)
    return pl.pallas_call(
        functools.partial(add_kernel, offsets, cuts),
        out_shape=tuple(pltpu.VMEM((n, *arrays[0].shape[1:]), BF16) for n in cuts),
        in_specs=[IN_VMEM] * len(arrays),
        out_specs=tuple(IN_VMEM for _ in cuts),
        compiler_params=PARAMS,
        cost_estimate=cost,
    )(*arrays)


def kept_basis(kept):
    freq = kept.astype(F32)[:, None]
    place = jnp.arange(SPAN).astype(F32)[None, :]
    scale = jnp.where(kept == 0, math.sqrt(1.0 / SPAN), math.sqrt(2.0 / SPAN)).astype(F32)
    return scale[:, None] * jnp.cos(math.pi * (2.0 * place + 1.0) * freq / (2.0 * SPAN))


def dot(a, b):
    return jnp.dot(a, b, precision=HIGH, preferred_element_type=F32)


def turned(a, b):
    return lax.dot_general(a, b, (((1,), (1,)), ((), ())), precision=HIGH, preferred_element_type=F32)


def split(a):
    high = a.astype(BF16)
    return high, (a - high.astype(F32)).astype(BF16)


def pack(coeffs):
    half = coeffs.shape[0] // 2
    return jnp.concatenate([coeffs[:half], coeffs[half:]], axis=1)


def unpack(packed):
    half = packed.shape[1] // 2
    return jnp.concatenate([packed[:, :half], packed[:, half:]], axis=0)


def basis_kernel(basis_ref, momentum_ref, wide_ref, tall_ref, rows_ref, right_ref, left_ref, coeffs_ref):
    basis = basis_ref[...]
    k, n = basis.shape
    blocks = wide_ref.shape[0] // k
    wide = jnp.concatenate([jnp.concatenate([basis] * blocks, axis=1)] * blocks, axis=0)
    row = lax.broadcasted_iota(jnp.int32, wide.shape, 0) // k
    col = lax.broadcasted_iota(jnp.int32, wide.shape, 1) // n
    wide = jnp.where(row == col, wide, 0.0)
    tall = wide.T
    wide_ref[...] = wide
    tall_ref[...] = tall
    high, low = split(wide)
    rows_ref[...] = jnp.concatenate([high, low], axis=0)
    right_ref[...] = jnp.concatenate([high, high, low], axis=0)
    high, low = split(tall)
    left_ref[...] = jnp.concatenate([high, low, high], axis=1)
    coeffs_ref[...] = pack(turned(dot(wide, 0.9 * momentum_ref[0]), wide).T)


def along_rows(rows, block):
    both = jnp.dot(rows, block, preferred_element_type=F32)
    half = both.shape[0] // 2
    return both[:half] + both[half:]


def late_kernel(near_ref, away_ref, back_ref, wide_ref, rows_ref, near_out_ref, coeffs_ref):
    near_out_ref[0] = (near_ref[0].astype(F32) + back_ref[0].astype(F32)).astype(BF16)
    away = (away_ref[0].astype(F32) + back_ref[1].astype(F32)).astype(BF16)
    coeffs_ref[...] = pack(turned(along_rows(rows_ref[...], away), wide_ref[...]))


def sent_kernel(near_ref, back_ref, own_ref, other_ref, wide_ref, rows_ref, sent_ref):
    rows = rows_ref[...]
    kept = along_rows(rows, near_ref[0]) + along_rows(rows, back_ref[0])
    sent = (pack(turned(kept, wide_ref[...])) + own_ref[...] + other_ref[...]).astype(BF16)
    for r in range(sent_ref.shape[0]):
        sent_ref[r] = sent


def new_kernel(momentum_ref, near_ref, r2_ref, r1_ref, wide_ref, tall_ref, out_ref):
    grad = near_ref[0].astype(F32) + r2_ref[0].astype(F32) + r1_ref[0].astype(F32)
    moment = 0.9 * momentum_ref[0] + grad.T
    wide, tall = wide_ref[...], tall_ref[...]
    out_ref[0] = moment - dot(tall, dot(dot(dot(wide, moment), tall), wide))


def update_kernel(every_ref, right_ref, left_ref, update_ref):
    total = jnp.sum(every_ref[...].astype(F32), axis=0) * (4.0 / every_ref.shape[0])
    high, low = split(unpack(total).T)
    mean = jnp.concatenate([high, low, high], axis=1)
    high, low = split(jnp.dot(mean, right_ref[...], preferred_element_type=F32))
    mean = jnp.concatenate([high, high, low], axis=0)
    update_ref[...] = jnp.dot(left_ref[...], mean, preferred_element_type=F32)


def on_vmem(kernel, out_shape, *args, cost=None):
    return pl.pallas_call(
        kernel,
        out_shape=out_shape,
        in_specs=[IN_VMEM] * len(args),
        out_specs=jax.tree.map(lambda _: IN_VMEM, out_shape),
        compiler_params=PARAMS,
        cost_estimate=cost,
    )(*args)


def after(a, *others):
    return lax.optimization_barrier((a, *others))[0]


def on_device(tokens, grad_hidden, momentum, kept):
    rows = momentum.shape[1]
    cols = momentum.shape[2]
    n_dp = lax.axis_size("dp")
    me = lax.axis_index("fsdp").astype(jnp.int32).reshape(1)

    def swap(a, perm):
        return lax.ppermute(a, "fsdp", perm)

    def places(flip, group):
        return tuple((flip, p, q) for p, q in group)

    got, held, left = first_product(places(True, EARLY + LATE), me, tokens, grad_hidden)
    got = swap(got, CORE)
    basis = kept_basis(kept)
    kw = cols // SPAN * KEEP
    packed = pltpu.VMEM((kw // 2, kw * 2), F32)
    unit = pltpu.VMEM((1, cols, rows), BF16)
    wide, tall, in_rows, on_right, on_left, own_coeffs = on_vmem(
        basis_kernel,
        (
            pltpu.VMEM((kw, cols), F32),
            pltpu.VMEM((cols, kw), F32),
            pltpu.VMEM((2 * kw, cols), BF16),
            pltpu.VMEM((3 * kw, cols), BF16),
            pltpu.VMEM((cols, 3 * kw), BF16),
            packed,
        ),
        basis,
        momentum,
    )
    own = product(places(False, EARLY + LATE), me, after(left, own_coeffs), held)
    (early_away,) = add([(own, 0), (got, 0)], (4,))
    early_back = swap(early_away, X1)
    left = after(left, early_away)
    other = product(places(True, REST), me, left, held, LONG)
    got_rest = swap(other, CORE)
    (late_away,) = add([(own, 4), (after(got, other), 4)], (4,))
    late_back = swap(late_away, X1)
    own = product(places(False, REST), me, after(left, late_away), held, LONG)
    near3, near2, away3, away2 = add([(own, 0), (got_rest, 0), (early_back, 0)], (1, 1, 1, 1))
    back3 = swap(away3, X2)
    back2 = swap(away2, X2)
    (a3,) = add([(near3, 0), (back3, 0)], (1,))
    r3 = swap(a3, Z1)
    near, away = add([(own, 4), (got_rest, 4), (after(late_back, a3), 0)], (2, 2))
    late_back = swap(away, X2)
    (a2,) = add([(near2, 0), (after(back2, away), 0)], (1,))
    r2 = swap(a2, Z1)
    (away,) = add([(near, 1), (r3, 0)], (1,), LONG)

    b0, coeffs = on_vmem(late_kernel, (unit, packed), near, away, late_back, wide, in_rows)
    (away,) = add([(away, 0), (after(late_back, coeffs), 1)], (1,), LONG)
    coeffs = swap(coeffs, Z2)
    r1 = swap(away, Z2)
    sent_shape = pltpu.VMEM((n_dp, kw // 2, kw * 2), BF16)
    sent = on_vmem(sent_kernel, sent_shape, b0, r2, own_coeffs, coeffs, wide, in_rows, cost=LONG)
    every = lax.all_to_all(sent, "dp", 0, 0, tiled=True)
    new_shape = jax.ShapeDtypeStruct((1, rows, cols), F32)
    new_momentum = on_vmem(new_kernel, new_shape, momentum, b0, r2, r1, wide, tall, cost=LONG)
    update = on_vmem(update_kernel, jax.ShapeDtypeStruct((rows, cols), F32), every, on_right, on_left)
    return new_momentum, update


def solution(mesh):
    in_specs = (P(("dp", "fsdp"), None), P(("dp", "fsdp"), None), P("dp", "fsdp", None), P())
    out_specs = (P("dp", "fsdp", None), P("fsdp", None))
    return jax.shard_map(
        on_device, mesh=mesh, in_specs=in_specs, out_specs=out_specs, check_vma=False
    )
```

```python
import functools
import math

import jax
import jax.numpy as jnp
from jax import lax
from jax.experimental import pallas as pl
from jax.experimental.pallas import tpu as pltpu
from jax.sharding import PartitionSpec as P

SPAN = 64
KEEP = 16
UNIT = 256
RING = 4
VMEM_LIMIT = 8 << 20
HIGH = lax.Precision.HIGHEST
BF16 = jnp.bfloat16
F32 = jnp.float32

MASKS = ((0, 3, 1, 2), (0, 1, 3, 2))

EARLY = tuple((p, q) for p in (2, 3) for q in (3, 2))
LATE = tuple((p, q) for p in (2, 3) for q in (0, 1))
REST = tuple((p, q) for p in (0, 1) for q in (3, 2)) + tuple((p, q) for p in (0, 1) for q in (0, 1))


def pairs(step):
    out = []
    for zh in range(RING):
        for x in range(RING):
            for c in range(2):
                a, b, d = step(zh, x, c)
                out.append(((zh * RING + x) * 2 + c, (a * RING + b) * 2 + d))
    return out


CORE = pairs(lambda zh, x, c: (zh, x, 1 - c))
X1 = pairs(lambda zh, x, c: (zh, x ^ MASKS[1 - c][2], c))
X2 = pairs(lambda zh, x, c: (zh, x ^ MASKS[1 - c][1], c))
Z1 = pairs(lambda zh, x, c: (zh ^ MASKS[c][2], x, c))
Z2 = pairs(lambda zh, x, c: (zh ^ MASKS[c][1], x, c))

LONG = pl.CostEstimate(flops=20_000_000_000, bytes_accessed=0, transcendentals=0)
IN_VMEM = pl.BlockSpec(memory_space=pltpu.VMEM)
PARAMS = pltpu.CompilerParams(vmem_limit_bytes=VMEM_LIMIT)


def block_start(me, flip, p, q):
    c = me % 2
    x = (me // 2) % RING
    zh = me // (2 * RING)
    if flip:
        c = 1 - c
    mx = jnp.where(c == 0, MASKS[1][p], MASKS[0][p])
    mz = jnp.where(c == 0, MASKS[0][q], MASKS[1][q])
    return pl.multiple_of((((zh ^ mz) * RING + (x ^ mx)) * 2 + c) * UNIT, UNIT)


def times(left, right):
    return jnp.dot(left, right, preferred_element_type=F32).astype(BF16)


def first_kernel(places, me_ref, tokens_ref, hidden_ref, out_ref, held_ref, left_ref, hidden, sems, hidden_sem):
    of_hidden = pltpu.make_async_copy(hidden_ref, hidden, hidden_sem)
    of_hidden.start()
    copies = []
    n = sems.shape[0]
    rows = tokens_ref.shape[0] // n
    for i in range(n):
        part = pl.ds(i * rows, rows)
        copy = pltpu.make_async_copy(tokens_ref.at[part], held_ref.at[part], sems.at[i])
        copy.start()
        copies.append(copy)
    of_hidden.wait()
    left = hidden[...].T
    left_ref[...] = left
    for copy in copies:
        copy.wait()
    for u, place in enumerate(places):
        out_ref[u] = times(left, held_ref[:, pl.ds(block_start(me_ref[0], *place), UNIT)])


def first_product(places, me, tokens, grad_hidden):
    toks, cols = grad_hidden.shape
    tokens = pltpu.with_memory_space_constraint(tokens, pltpu.HBM)
    grad_hidden = pltpu.with_memory_space_constraint(grad_hidden, pltpu.HBM)
    hbm = pl.BlockSpec(memory_space=pltpu.HBM)
    return pl.pallas_call(
        functools.partial(first_kernel, places),
        out_shape=(
            pltpu.VMEM((len(places), cols, UNIT), BF16),
            pltpu.VMEM(tokens.shape, BF16),
            pltpu.VMEM((cols, toks), BF16),
        ),
        in_specs=[pl.BlockSpec(memory_space=pltpu.SMEM), hbm, hbm],
        out_specs=(IN_VMEM, IN_VMEM, IN_VMEM),
        scratch_shapes=[
            pltpu.VMEM((toks, cols), BF16),
            pltpu.SemaphoreType.DMA((4,)),
            pltpu.SemaphoreType.DMA,
        ],
        compiler_params=PARAMS,
    )(me, tokens, grad_hidden)


def product_kernel(places, me_ref, left_ref, held_ref, out_ref):
    left = left_ref[...]
    for u, place in enumerate(places):
        out_ref[u] = times(left, held_ref[:, pl.ds(block_start(me_ref[0], *place), UNIT)])


def product(places, me, left, held, cost=None):
    cols, toks = left.shape
    return pl.pallas_call(
        functools.partial(product_kernel, places),
        out_shape=pltpu.VMEM((len(places), cols, UNIT), BF16),
        in_specs=[pl.BlockSpec(memory_space=pltpu.SMEM), IN_VMEM, IN_VMEM],
        out_specs=IN_VMEM,
        compiler_params=PARAMS,
        cost_estimate=cost,
    )(me, left, held)


def add_kernel(offsets, cuts, *refs):
    in_refs, out_refs = refs[: len(offsets)], refs[len(offsets) :]
    at = 0
    for out_ref, n in zip(out_refs, cuts, strict=True):
        for u in range(n):
            total = in_refs[0][offsets[0] + at + u].astype(F32)
            for in_ref, offset in zip(in_refs[1:], offsets[1:], strict=True):
                total += in_ref[offset + at + u].astype(F32)
            out_ref[u] = total.astype(BF16)
        at += n


def add(terms, cuts, cost=None):
    arrays, offsets = zip(*terms, strict=True)
    return pl.pallas_call(
        functools.partial(add_kernel, offsets, cuts),
        out_shape=tuple(pltpu.VMEM((n, *arrays[0].shape[1:]), BF16) for n in cuts),
        in_specs=[IN_VMEM] * len(arrays),
        out_specs=tuple(IN_VMEM for _ in cuts),
        compiler_params=PARAMS,
        cost_estimate=cost,
    )(*arrays)


def kept_basis(kept):
    freq = kept.astype(F32)[:, None]
    place = jnp.arange(SPAN).astype(F32)[None, :]
    scale = jnp.where(kept == 0, math.sqrt(1.0 / SPAN), math.sqrt(2.0 / SPAN)).astype(F32)
    return scale[:, None] * jnp.cos(math.pi * (2.0 * place + 1.0) * freq / (2.0 * SPAN))


def dot(a, b):
    return jnp.dot(a, b, precision=HIGH, preferred_element_type=F32)


def turned(a, b):
    return lax.dot_general(a, b, (((1,), (1,)), ((), ())), precision=HIGH, preferred_element_type=F32)


def split(a):
    high = a.astype(BF16)
    return high, (a - high.astype(F32)).astype(BF16)


def pack(coeffs):
    half = coeffs.shape[0] // 2
    return jnp.concatenate([coeffs[:half], coeffs[half:]], axis=1)


def unpack(packed):
    half = packed.shape[1] // 2
    return jnp.concatenate([packed[:, :half], packed[:, half:]], axis=0)


def basis_kernel(basis_ref, momentum_ref, wide_ref, tall_ref, rows_ref, right_ref, left_ref, coeffs_ref):
    basis = basis_ref[...]
    k, n = basis.shape
    blocks = wide_ref.shape[0] // k
    wide = jnp.concatenate([jnp.concatenate([basis] * blocks, axis=1)] * blocks, axis=0)
    row = lax.broadcasted_iota(jnp.int32, wide.shape, 0) // k
    col = lax.broadcasted_iota(jnp.int32, wide.shape, 1) // n
    wide = jnp.where(row == col, wide, 0.0)
    tall = wide.T
    wide_ref[...] = wide
    tall_ref[...] = tall
    high, low = split(wide)
    rows_ref[...] = jnp.concatenate([high, low], axis=0)
    right_ref[...] = jnp.concatenate([high, high, low], axis=0)
    high, low = split(tall)
    left_ref[...] = jnp.concatenate([high, low, high], axis=1)
    coeffs_ref[...] = pack(turned(dot(wide, 0.9 * momentum_ref[0]), wide))


def along_rows(rows, block):
    both = jnp.dot(rows, block, preferred_element_type=F32)
    half = both.shape[0] // 2
    return both[:half] + both[half:]


def late_kernel(near_ref, away_ref, back_ref, wide_ref, rows_ref, near_out_ref, coeffs_ref):
    near_out_ref[0] = (near_ref[0].astype(F32) + back_ref[0].astype(F32)).astype(BF16)
    away = (away_ref[0].astype(F32) + back_ref[1].astype(F32)).astype(BF16)
    coeffs_ref[...] = pack(turned(wide_ref[...], along_rows(rows_ref[...], away)))


def sent_kernel(near_ref, back_ref, own_ref, other_ref, wide_ref, rows_ref, sent_ref):
    rows = rows_ref[...]
    kept = along_rows(rows, near_ref[0]) + along_rows(rows, back_ref[0])
    sent = (pack(turned(wide_ref[...], kept)) + own_ref[...] + other_ref[...]).astype(BF16)
    for r in range(sent_ref.shape[0]):
        sent_ref[r] = sent


def new_kernel(momentum_ref, near_ref, r2_ref, r1_ref, wide_ref, tall_ref, out_ref):
    grad = near_ref[0].astype(F32) + r2_ref[0].astype(F32) + r1_ref[0].astype(F32)
    moment = 0.9 * momentum_ref[0] + grad.T
    wide, tall = wide_ref[...], tall_ref[...]
    out_ref[0] = moment - dot(tall, dot(dot(dot(wide, moment), tall), wide))


def update_kernel(every_ref, right_ref, left_ref, update_ref):
    total = jnp.sum(every_ref[...].astype(F32), axis=0) * (4.0 / every_ref.shape[0])
    high, low = split(unpack(total))
    mean = jnp.concatenate([high, low, high], axis=1)
    high, low = split(jnp.dot(mean, right_ref[...], preferred_element_type=F32))
    mean = jnp.concatenate([high, high, low], axis=0)
    update_ref[...] = jnp.dot(left_ref[...], mean, preferred_element_type=F32)


def on_vmem(kernel, out_shape, *args, cost=None):
    return pl.pallas_call(
        kernel,
        out_shape=out_shape,
        in_specs=[IN_VMEM] * len(args),
        out_specs=jax.tree.map(lambda _: IN_VMEM, out_shape),
        compiler_params=PARAMS,
        cost_estimate=cost,
    )(*args)


def after(a, *others):
    return lax.optimization_barrier((a, *others))[0]


def on_device(tokens, grad_hidden, momentum, kept):
    rows = momentum.shape[1]
    cols = momentum.shape[2]
    n_dp = lax.axis_size("dp")
    me = lax.axis_index("fsdp").astype(jnp.int32).reshape(1)

    def swap(a, perm):
        return lax.ppermute(a, "fsdp", perm)

    def places(flip, group):
        return tuple((flip, p, q) for p, q in group)

    got, held, left = first_product(places(True, EARLY + LATE), me, tokens, grad_hidden)
    got = swap(got, CORE)
    basis = kept_basis(kept)
    kw = cols // SPAN * KEEP
    packed = pltpu.VMEM((kw // 2, kw * 2), F32)
    unit = pltpu.VMEM((1, cols, rows), BF16)
    wide, tall, in_rows, on_right, on_left, own_coeffs = on_vmem(
        basis_kernel,
        (
            pltpu.VMEM((kw, cols), F32),
            pltpu.VMEM((cols, kw), F32),
            pltpu.VMEM((2 * kw, cols), BF16),
            pltpu.VMEM((3 * kw, cols), BF16),
            pltpu.VMEM((cols, 3 * kw), BF16),
            packed,
        ),
        basis,
        momentum,
    )
    own = product(places(False, EARLY + LATE), me, after(left, own_coeffs), held)
    (early_away,) = add([(own, 0), (got, 0)], (4,))
    early_back = swap(early_away, X1)
    left = after(left, early_away)
    other = product(places(True, REST), me, left, held, LONG)
    got_rest = swap(other, CORE)
    (late_away,) = add([(own, 4), (after(got, other), 4)], (4,))
    late_back = swap(late_away, X1)
    own = product(places(False, REST), me, after(left, late_away), held, LONG)
    near3, near2, away3, away2 = add([(own, 0), (got_rest, 0), (early_back, 0)], (1, 1, 1, 1))
    back3 = swap(away3, X2)
    back2 = swap(away2, X2)
    (a3,) = add([(near3, 0), (back3, 0)], (1,))
    near, away = add([(own, 4), (got_rest, 4), (late_back, 0)], (2, 2))
    late_back = swap(away, X2)
    r3 = swap(after(a3, away), Z1)
    (a2,) = add([(near2, 0), (after(back2, away), 0)], (1,))
    r2 = swap(a2, Z1)
    (away,) = add([(near, 1), (r3, 0)], (1,), LONG)

    b0, coeffs = on_vmem(late_kernel, (unit, packed), near, away, late_back, wide, in_rows)
    (away,) = add([(away, 0), (after(late_back, coeffs), 1)], (1,), LONG)
    coeffs = swap(coeffs, Z2)
    r1 = swap(away, Z2)
    sent_shape = pltpu.VMEM((n_dp, kw // 2, kw * 2), BF16)
    sent = on_vmem(sent_kernel, sent_shape, b0, r2, own_coeffs, coeffs, wide, in_rows, cost=LONG)
    every = lax.all_to_all(sent, "dp", 0, 0, tiled=True)
    new_shape = jax.ShapeDtypeStruct((1, rows, cols), F32)
    new_momentum = on_vmem(new_kernel, new_shape, momentum, b0, r2, r1, wide, tall, cost=LONG)
    update = on_vmem(update_kernel, jax.ShapeDtypeStruct((rows, cols), F32), every, on_right, on_left)
    return new_momentum, update


def solution(mesh):
    in_specs = (P(("dp", "fsdp"), None), P(("dp", "fsdp"), None), P("dp", "fsdp", None), P())
    out_specs = (P("dp", "fsdp", None), P("fsdp", None))
    return jax.shard_map(
        on_device, mesh=mesh, in_specs=in_specs, out_specs=out_specs, check_vma=False
    )
```
